512 devices in a mesh: prow: 16 (over y, x), pcol: 32 (over z, core).
Axes of the slice: x: 4, y: 4, z: 16, core: 2. Of those that a mesh axis runs over, the one named last changes fastest.
Arguments:
- panel: float32 [65536, 128], P(('prow', 'pcol')), may hold values from -0.0234375 to 0.0234375
- solved: float32 [65536, 8192], P('prow', 'pcol'), may hold values from -6 to 6
- window_rhs: float32 [128, 8192], P('prow', 'pcol'), may hold values from -6 to 6
- coupling: float32 [64, 64], replicated, may hold values from -0.75 to 0.75
- inverses: float32 [2, 64, 64], replicated, may hold values from -0.5 to 1.4, as said below
Outputs:
- window_z: float32 [128, 8192], P('prow', 'pcol')
The draws below stay inside these ranges and needn't reach their ends.
Inputs may be any that keep to these rules, and one draw needn't show every extreme that they name: `inverses`: each of the two tiles is lower triangular with a positive diagonal.
All inputs are finite; a program needn't handle non-finite values.
Results may differ from the reference program's by a relative error of at most 0.00007.
Values sent between devices are 32-bit elements; how exact they have to be, the bound alone decides.
No kernel may reach another device: no remote copies, remote signals or barrier semaphores. Data moves between devices by JAX's collectives and lax.ppermute only.
A program may use at most 64 MiB of HBM per device.

```python
import jax
import jax.numpy as jnp
from jax import lax

BLOCK = 64
PANEL = 128
BELOW = 65536
RHS = 8192


def draw_inverses(key, part):
    key = jax.random.fold_in(key, 5)
    key_lower, key_diag = jax.random.split(key)
    lower = jax.random.normal(key_lower, (2, BLOCK, BLOCK), jnp.float32) * 0.1
    lower = jnp.tril(jnp.clip(lower, -0.5, 0.5), -1)
    diag_values = jax.random.uniform(key_diag, (2, BLOCK), jnp.float32, 0.6, 1.4)
    return lower + diag_values[:, :, None] * jnp.eye(BLOCK, dtype=jnp.float32)[None]


def shard_levels(stream_key, extent, cuts, low, largest):
    gain, own = 1.0, jax.random.fold_in(stream_key, 6)
    for position, blocks in cuts:
        steps = jnp.exp(jax.random.uniform(jax.random.fold_in(own, position), (blocks,), jnp.float32, low / len(cuts), largest / len(cuts)))
        gain = gain * jnp.repeat(steps, extent[position] // blocks).reshape([-1 if axis == position else 1 for axis in range(len(extent))])
    return gain


def gaussian(rng, shape, scale, most, cuts=(), kind=jnp.bfloat16):
    array = scale * jax.random.normal(rng, shape, jnp.float32)
    if cuts:
        array = array * shard_levels(rng, shape, cuts, -0.22, 0.18)
    return jnp.clip(array, -most, most).astype(kind)


def setup_inputs(seed: int = 0) -> dict:
    key_list = jax.random.split(jax.random.key(seed), 6)
    return {
        "panel": gaussian(key_list[0], (BELOW, PANEL), BELOW ** -0.5, 0.0234375, ((0, 512),), jnp.float32),
        "solved": gaussian(key_list[1], (BELOW, RHS), 1.0, 6.0, ((0, 16), (1, 32)), jnp.float32),
        "window_rhs": gaussian(key_list[2], (PANEL, RHS), 1.0, 6.0, ((0, 16), (1, 32)), jnp.float32),
        "coupling": gaussian(key_list[3], (BLOCK, BLOCK), BLOCK ** -0.5, 0.75, (), jnp.float32),
        "inverses": draw_inverses(jax.random.fold_in(key_list[5], 71), 0),
    }


def reference(panel, solved, window_rhs, coupling, inverses):
    update = jnp.dot(panel.T, solved, precision=lax.Precision.HIGHEST, preferred_element_type=jnp.float32)
    remainder = window_rhs - update
    later_block = jnp.dot(inverses[1].T, remainder[BLOCK:], precision=lax.Precision.HIGHEST, preferred_element_type=jnp.float32)
    carried = remainder[:BLOCK] - jnp.dot(coupling.T, later_block, precision=lax.Precision.HIGHEST, preferred_element_type=jnp.float32)
    first_block = jnp.dot(inverses[0].T, carried, precision=lax.Precision.HIGHEST, preferred_element_type=jnp.float32)
    return jnp.concatenate([first_block, later_block], axis=0)
```

```python
import jax
import jax.numpy as jnp
from jax import lax
from jax.sharding import PartitionSpec as P

GATHERED = 120


def transposed_product(left, right, precision=lax.Precision.HIGHEST):
    return lax.dot_general(
        left,
        right,
        (((0,), (0,)), ((), ())),
        precision=precision,
        preferred_element_type=jnp.float32,
    )


def body(panel, solved, window_rhs, coupling, inverses):
    block_rows = coupling.shape[0]
    share_rows = window_rhs.shape[0]
    panel_rows, panel_columns = panel.shape
    columns = window_rhs.shape[1]
    grid_rows = lax.axis_size("prow")
    grid_columns = lax.axis_size("pcol")
    chips = grid_columns // 2
    row_index = lax.axis_index("prow")
    core = lax.axis_index("pcol") % 2
    same_core = [[2 * z + c for z in range(chips)] for c in range(2)]
    rest = jnp.broadcast_to(panel[None, GATHERED:], (chips, panel_rows - GATHERED, panel_columns))
    rest = lax.all_to_all(rest, "pcol", 0, 0, axis_index_groups=same_core)
    most = lax.all_gather(panel[:GATHERED], "pcol", axis=0, axis_index_groups=same_core)
    own = jnp.concatenate([most, rest], axis=1).reshape(chips * panel_rows, panel_columns)
    other = lax.ppermute(own, "pcol", [(i, i ^ 1) for i in range(grid_columns)])
    tiles = solved.reshape(chips, 2, panel_rows, columns)
    own_rows = lax.dynamic_index_in_dim(tiles, core, 1, False).reshape(-1, columns)
    other_rows = lax.dynamic_index_in_dim(tiles, 1 - core, 1, False).reshape(-1, columns)
    update = transposed_product(own, own_rows, lax.Precision.HIGH)
    update = update + transposed_product(other, other_rows, lax.Precision.HIGH)
    negated = -update
    own_start = row_index * share_rows
    own_part = lax.dynamic_slice_in_dim(negated, own_start, share_rows, 0) + window_rhs
    remainder = lax.dynamic_update_slice_in_dim(negated, own_part, own_start, 0)
    later_block = transposed_product(inverses[1], remainder[block_rows:])
    carried = remainder[:block_rows] - transposed_product(coupling, later_block)
    first_block = transposed_product(inverses[0], carried)
    window_z = jnp.concatenate([first_block, later_block], axis=0)
    parts = window_z.reshape(grid_rows, share_rows, columns)
    return jnp.sum(lax.all_to_all(parts, "prow", 0, 0), axis=0)


def solution(mesh):
    placed = (P(("prow", "pcol"), None), P("prow", "pcol"), P("prow", "pcol"), P(), P())
    return jax.shard_map(
        body, mesh=mesh, in_specs=placed, out_specs=P("prow", "pcol"), check_vma=False
    )
```

```python
import jax
import jax.numpy as jnp
from jax import lax
from jax.sharding import PartitionSpec as P

STRIDE = 4


def transposed_product(left, right, precision=lax.Precision.HIGHEST):
    return lax.dot_general(
        left,
        right,
        (((0,), (0,)), ((), ())),
        precision=precision,
        preferred_element_type=jnp.float32,
    )


def body(panel, solved, window_rhs, coupling, inverses):
    block_rows = coupling.shape[0]
    share_rows, columns = window_rhs.shape
    panel_rows, panel_columns = panel.shape
    grid_rows = lax.axis_size("prow")
    grid_columns = lax.axis_size("pcol")
    chips = grid_columns // 2
    far = chips // STRIDE
    row_index = lax.axis_index("prow")
    column_index = lax.axis_index("pcol")
    core = column_index % 2
    place = (column_index // 2) % STRIDE

    def shifted(array, up, down):
        pairs = [(2 * z + c, 2 * ((z + (up, down)[c]) % chips) + c) for z in range(chips) for c in range(2)]
        return lax.ppermute(array, "pcol", pairs)

    def swapped(array):
        return lax.ppermute(array, "pcol", [(i, i ^ 1) for i in range(grid_columns)])

    groups = [[2 * (STRIDE * h + l) + c for h in range(far)] for l in range(STRIDE) for c in range(2)]
    own = lax.all_gather(panel, "pcol", axis=0, axis_index_groups=groups, tiled=True)
    bundles = [own, shifted(own, 1, 1), shifted(own, -1, -1), shifted(own, 2, -2)]
    offsets = [0, -1, 1, 2]
    tiles = solved.reshape(far, STRIDE, 2, panel_rows, columns)

    def rows_of(offset, which):
        start = (0, (place + offset) % STRIDE, which, 0, 0)
        part = lax.dynamic_slice(tiles, start, (far, 1, 1, panel_rows, columns))
        return part.reshape(far * panel_rows, columns)

    update = 0.0
    for bundle, offset in zip(bundles, offsets):
        update += transposed_product(bundle, rows_of(offset, core), lax.Precision.HIGH)
        update += transposed_product(swapped(bundle), rows_of(offset, 1 - core), lax.Precision.HIGH)
    negated = -update
    own_start = row_index * share_rows
    own_part = lax.dynamic_slice_in_dim(negated, own_start, share_rows, 0) + window_rhs
    remainder = lax.dynamic_update_slice_in_dim(negated, own_part, own_start, 0)
    later_block = transposed_product(inverses[1], remainder[block_rows:])
    carried = remainder[:block_rows] - transposed_product(coupling, later_block)
    first_block = transposed_product(inverses[0], carried)
    window_z = jnp.concatenate([first_block, later_block], axis=0)
    parts = window_z.reshape(grid_rows, share_rows, columns)
    return jnp.sum(lax.all_to_all(parts, "prow", 0, 0), axis=0)


def solution(mesh):
    placed = (P(("prow", "pcol"), None), P("prow", "pcol"), P("prow", "pcol"), P(), P())
    return jax.shard_map(
        body, mesh=mesh, in_specs=placed, out_specs=P("prow", "pcol"), check_vma=False
    )
```

```python
import jax
import jax.numpy as jnp
from jax import lax
from jax.experimental import pallas as pl
from jax.experimental.pallas import tpu as pltpu
from jax.sharding import PartitionSpec as P

STRIDE = 4
WINDOW_FLOPS = 10_000_000_000
PARAMS = pltpu.CompilerParams(vmem_limit_bytes=20 << 20)


def transposed_product(left, right):
    return lax.dot_general(
        left,
        right,
        (((0,), (0,)), ((), ())),
        precision=lax.Precision.HIGHEST,
        preferred_element_type=jnp.float32,
    )


def halves(array):
    high = array.astype(jnp.bfloat16)
    return high, (array - high.astype(jnp.float32)).astype(jnp.bfloat16)


def three_passes(rows, right_high, right_low):
    left_high, left_low = halves(rows.T)
    total = jnp.dot(left_high, right_high, preferred_element_type=jnp.float32)
    total += jnp.dot(left_high, right_low, preferred_element_type=jnp.float32)
    return total + jnp.dot(left_low, right_high, preferred_element_type=jnp.float32)


def first_kernel(where, rows, s_own, s_near, s_far, s_away, s_gone, out, n_high, n_low, a_high, a_low):
    columns = out.shape[1]
    part = three_passes(rows[...], *halves(s_own[...].reshape(-1, columns)))

    @pl.when(pl.program_id(0) == 0)
    def _():
        out[...] = part

    @pl.when(pl.program_id(0) > 0)
    def _():
        out[...] += part

    for index, source in enumerate((s_near, s_far)):
        n_high[index], n_low[index] = halves(source[...].reshape(-1, columns))
    for index, source in enumerate((s_away, s_gone)):
        a_high[index], a_low[index] = halves(source[...].reshape(-1, columns))


def first_product(where, rows, tiles):
    far, _, cores, panel_rows, columns = tiles.shape
    panel_columns = rows.shape[1]
    pair = cores * panel_rows

    def two(which):
        return pl.BlockSpec((None, None, cores, panel_rows, columns), lambda h, s: (h, s[which], 0, 0, 0))

    def one(which):
        return pl.BlockSpec((None, None, None, panel_rows, columns), lambda h, s: (h, s[2], s[which], 0, 0))

    def split(depth):
        shape = jax.ShapeDtypeStruct((2, far * depth, columns), jnp.bfloat16)
        return [shape] * 2, [pl.BlockSpec((2, depth, columns), lambda h, s: (0, h, 0))] * 2

    near_shapes, near_specs = split(pair)
    away_shapes, away_specs = split(panel_rows)
    return pl.pallas_call(
        first_kernel,
        out_shape=[jax.ShapeDtypeStruct((panel_columns, columns), jnp.float32)] + near_shapes + away_shapes,
        grid_spec=pltpu.PrefetchScalarGridSpec(
            num_scalar_prefetch=1,
            grid=(far,),
            in_specs=[pl.BlockSpec((pair, panel_columns), lambda h, s: (h, 0))]
            + [two(0), two(1), two(5), one(3), one(6)],
            out_specs=[pl.BlockSpec((panel_columns, columns), lambda h, s: (0, 0))] + near_specs + away_specs,
        ),
        compiler_params=PARAMS,
        cost_estimate=pl.CostEstimate(flops=WINDOW_FLOPS, bytes_accessed=8 << 20, transcendentals=0),
    )(where, rows, *[tiles] * 5)


def add_kernel(index, near, away, sofar, n_high, n_low, a_high, a_low, out):
    out[...] = (
        sofar[...]
        + three_passes(near[...], n_high[index], n_low[index])
        + three_passes(away[...], a_high[index], a_low[index])
    )


def middle_product(near, away, sofar, split):
    return pl.pallas_call(
        lambda *refs: add_kernel(0, *refs),
        out_shape=jax.ShapeDtypeStruct(sofar.shape, jnp.float32),
        compiler_params=PARAMS,
        cost_estimate=pl.CostEstimate(flops=3 << 26, bytes_accessed=3 << 20, transcendentals=0),
    )(near, away, sofar, *split)


def last_kernel(where, near, away, sofar, n_high, n_low, a_high, a_low, rhs, coupling, inverses, out, total):
    share_rows, columns = rhs.shape
    block_rows = coupling.shape[0]
    add_kernel(1, near, away, sofar, n_high, n_low, a_high, a_low, total)
    total[...] = -total[...]
    at = pl.ds(pl.multiple_of(where[4] * share_rows, share_rows), share_rows)
    total[at, :] += rhs[...]
    later = transposed_product(inverses[1], total[block_rows:, :])
    carried = total[:block_rows, :] - transposed_product(coupling[...], later)
    count = block_rows // share_rows
    out[count:] = later.reshape(count, share_rows, columns)
    out[:count] = transposed_product(inverses[0], carried).reshape(count, share_rows, columns)


def last_product(where, near, away, sofar, split, rhs, coupling, inverses):
    panel_columns, columns = sofar.shape
    share_rows = rhs.shape[0]
    out_shape = (panel_columns // share_rows, share_rows, columns)
    vmem = pl.BlockSpec(memory_space=pltpu.VMEM)
    return pl.pallas_call(
        last_kernel,
        out_shape=jax.ShapeDtypeStruct(out_shape, jnp.float32),
        in_specs=[pl.BlockSpec(memory_space=pltpu.SMEM)] + [vmem] * 10,
        scratch_shapes=[pltpu.VMEM(sofar.shape, jnp.float32)],
        compiler_params=PARAMS,
        cost_estimate=pl.CostEstimate(flops=3 << 26, bytes_accessed=3 << 20, transcendentals=0),
    )(where, near, away, sofar, *split, rhs, coupling, inverses)


def body(panel, solved, window_rhs, coupling, inverses):
    columns = window_rhs.shape[1]
    panel_rows, panel_columns = panel.shape
    grid_columns = lax.axis_size("pcol")
    chips = grid_columns // 2
    far = chips // STRIDE
    row_index = lax.axis_index("prow")
    column_index = lax.axis_index("pcol")
    core = column_index % 2
    place = (column_index // 2) % STRIDE
    tiles = solved.reshape(far, STRIDE, 2, panel_rows, columns)
    tiles = pltpu.with_memory_space_constraint(tiles, pltpu.HBM)

    def shifted(array, up, down):
        pairs = [(2 * z + c, 2 * ((z + (up, down)[c]) % chips) + c) for z in range(chips) for c in range(2)]
        return lax.ppermute(array, "pcol", pairs)

    def swapped(array):
        return lax.ppermute(array, "pcol", [(i, i ^ 1) for i in range(grid_columns)])

    groups = [[2 * (STRIDE * h + l) + c for h in range(far) for c in range(2)] for l in range(STRIDE)]
    own = lax.all_gather(panel, "pcol", axis=0, axis_index_groups=groups, tiled=True)
    near = shifted(own, 1, -1)
    by_core = own.reshape(far, 2, panel_rows, panel_columns)
    away = lax.dynamic_index_in_dim(by_core, core, 1, False).reshape(far * panel_rows, panel_columns)
    away = shifted(away, 2, -2)
    below, above = (place + STRIDE - 1) % STRIDE, (place + 1) % STRIDE
    near_place = jnp.where(core == 0, below, above)
    far_place = jnp.where(core == 0, above, below)
    where = [place, near_place, (place + 2) % STRIDE, core, row_index, far_place, 1 - core]
    where = jnp.stack(where).astype(jnp.int32)
    near, away, (sofar, *split) = lax.optimization_barrier((near, away, first_product(where, own, tiles)))
    other_near, other_away = swapped(near), swapped(away)
    sofar = middle_product(near, away, sofar, split)
    parts = last_product(where, other_near, other_away, sofar, split, window_rhs, coupling, inverses)
    return jnp.sum(lax.all_to_all(parts, "prow", 0, 0), axis=0)


def solution(mesh):
    placed = (P(("prow", "pcol"), None), P("prow", "pcol"), P("prow", "pcol"), P(), P())
    return jax.shard_map(
        body, mesh=mesh, in_specs=placed, out_specs=P("prow", "pcol"), check_vma=False
    )
```

```python
import jax
import jax.numpy as jnp
from jax import lax
from jax.experimental import pallas as pl
from jax.experimental.pallas import tpu as pltpu
from jax.sharding import PartitionSpec as P

STRIDE = 4
WINDOW_FLOPS = 10_000_000_000
PARAMS = pltpu.CompilerParams(vmem_limit_bytes=20 << 20)


def transposed_product(left, right):
    return lax.dot_general(
        left,
        right,
        (((0,), (0,)), ((), ())),
        precision=lax.Precision.HIGHEST,
        preferred_element_type=jnp.float32,
    )


def halves(array):
    high = array.astype(jnp.bfloat16)
    return high, (array - high.astype(jnp.float32)).astype(jnp.bfloat16)


def three_passes(rows, right_high, right_low):
    left_high, left_low = halves(rows.T)
    total = jnp.dot(left_high, right_high, preferred_element_type=jnp.float32)
    total += jnp.dot(left_high, right_low, preferred_element_type=jnp.float32)
    return total + jnp.dot(left_low, right_high, preferred_element_type=jnp.float32)


def plain_product(left, right):
    return jnp.dot(left, right, precision=lax.Precision.HIGHEST, preferred_element_type=jnp.float32)


def first_kernel(
    where, rows, s_own, s_near, s_far, s_away, s_gone, coupling, inverses, out, n_high, n_low, a_high, a_low, solve
):
    columns = out.shape[1]
    part = three_passes(rows[...], *halves(s_own[...].reshape(-1, columns)))

    @pl.when(pl.program_id(0) == 0)
    def _():
        out[...] = part

    @pl.when(pl.program_id(0) > 0)
    def _():
        out[...] += part

    @pl.when(pl.program_id(0) == 0)
    def _():
        upper, lower = inverses[0], inverses[1]
        carried = -plain_product(lower, plain_product(coupling[...], upper))
        top = jnp.concatenate([upper.T, carried.T], axis=1)
        bottom = jnp.concatenate([jnp.zeros_like(lower), lower.T], axis=1)
        solve[...] = jnp.concatenate([top, bottom], axis=0)

    for index, source in enumerate((s_near, s_far)):
        n_high[index], n_low[index] = halves(source[...].reshape(-1, columns))
    for index, source in enumerate((s_away, s_gone)):
        a_high[index], a_low[index] = halves(source[...].reshape(-1, columns))


def whole(array):
    return pl.BlockSpec(array.shape, lambda h, s: (0,) * array.ndim)


def first_product(where, rows, tiles, coupling, inverses):
    far, _, cores, panel_rows, columns = tiles.shape
    panel_columns = rows.shape[1]
    pair = cores * panel_rows

    def two(which):
        return pl.BlockSpec((None, None, cores, panel_rows, columns), lambda h, s: (h, s[which], 0, 0, 0))

    def one(which):
        return pl.BlockSpec((None, None, None, panel_rows, columns), lambda h, s: (h, s[2], s[which], 0, 0))

    def split(depth):
        shape = jax.ShapeDtypeStruct((2, far * depth, columns), jnp.bfloat16)
        return [shape] * 2, [pl.BlockSpec((2, depth, columns), lambda h, s: (0, h, 0))] * 2

    near_shapes, near_specs = split(pair)
    away_shapes, away_specs = split(panel_rows)
    return pl.pallas_call(
        first_kernel,
        out_shape=[jax.ShapeDtypeStruct((panel_columns, columns), jnp.float32)]
        + near_shapes
        + away_shapes
        + [jax.ShapeDtypeStruct((panel_columns, panel_columns), jnp.float32)],
        grid_spec=pltpu.PrefetchScalarGridSpec(
            num_scalar_prefetch=1,
            grid=(far,),
            in_specs=[pl.BlockSpec((pair, panel_columns), lambda h, s: (h, 0))]
            + [two(0), two(1), two(5), one(3), one(6), whole(coupling), whole(inverses)],
            out_specs=[pl.BlockSpec((panel_columns, columns), lambda h, s: (0, 0))]
            + near_specs
            + away_specs
            + [pl.BlockSpec((panel_columns, panel_columns), lambda h, s: (0, 0))],
        ),
        compiler_params=PARAMS,
        cost_estimate=pl.CostEstimate(flops=WINDOW_FLOPS, bytes_accessed=8 << 20, transcendentals=0),
    )(where, rows, *[tiles] * 5, coupling, inverses)


def call(kernel, out_shape, where, *arrays, scratch=()):
    return pl.pallas_call(
        kernel,
        out_shape=jax.ShapeDtypeStruct(out_shape, jnp.float32),
        in_specs=[pl.BlockSpec(memory_space=pltpu.SMEM)] + [pl.BlockSpec(memory_space=pltpu.VMEM)] * len(arrays),
        scratch_shapes=scratch,
        compiler_params=PARAMS,
        cost_estimate=pl.CostEstimate(flops=3 << 26, bytes_accessed=1 << 20, transcendentals=0),
    )(where, *arrays)


def middle_kernel(where, near, away, sofar, n_high, n_low, a_high, a_low, rhs, solve, out, total):
    share_rows = rhs.shape[0]
    total[...] = -sofar[...] - three_passes(near[...], n_high[0], n_low[0])
    total[...] -= three_passes(away[...], a_high[0], a_low[0])
    at = pl.ds(pl.multiple_of(where[4] * share_rows, share_rows), share_rows)
    total[at, :] += rhs[...]
    out[...] = plain_product(solve[...], total[...])


def last_kernel(where, other, sofar, n_high, n_low, a_high, a_low, solve, out):
    depth = n_high.shape[1]
    update = three_passes(other[0:depth, :], n_high[1], n_low[1])
    update += three_passes(other[depth:, :], a_high[1], a_low[1])
    out[...] = (sofar[...] - plain_product(solve[...], update)).reshape(out.shape)


def body(panel, solved, window_rhs, coupling, inverses):
    columns = window_rhs.shape[1]
    panel_rows, panel_columns = panel.shape
    grid_columns = lax.axis_size("pcol")
    chips = grid_columns // 2
    far = chips // STRIDE
    row_index = lax.axis_index("prow")
    column_index = lax.axis_index("pcol")
    core = column_index % 2
    place = (column_index // 2) % STRIDE
    tiles = solved.reshape(far, STRIDE, 2, panel_rows, columns)
    tiles = pltpu.with_memory_space_constraint(tiles, pltpu.HBM)

    def shifted(array, up, down):
        pairs = [(2 * z + c, 2 * ((z + (up, down)[c]) % chips) + c) for z in range(chips) for c in range(2)]
        return lax.ppermute(array, "pcol", pairs)

    def swapped(array):
        return lax.ppermute(array, "pcol", [(i, i ^ 1) for i in range(grid_columns)])

    groups = [[2 * (STRIDE * h + l) + c for h in range(far) for c in range(2)] for l in range(STRIDE)]
    own = lax.all_gather(panel, "pcol", axis=0, axis_index_groups=groups, tiled=True)
    near = shifted(own, 1, -1)
    by_core = own.reshape(far, 2, panel_rows, panel_columns)
    away = lax.dynamic_index_in_dim(by_core, core, 1, False).reshape(far * panel_rows, panel_columns)
    away = shifted(away, 2, -2)
    below, above = (place + STRIDE - 1) % STRIDE, (place + 1) % STRIDE
    near_place = jnp.where(core == 0, below, above)
    far_place = jnp.where(core == 0, above, below)
    where = [place, near_place, (place + 2) % STRIDE, core, row_index, far_place, 1 - core]
    where = jnp.stack(where).astype(jnp.int32)
    work = first_product(where, own, tiles, coupling, inverses)
    near, away, (sofar, *split, solve) = lax.optimization_barrier((near, away, work))
    other = swapped(jnp.concatenate([near, away]))
    shape = sofar.shape
    sofar = call(
        middle_kernel, shape, where, near, away, sofar, *split, window_rhs, solve,
        scratch=[pltpu.VMEM(shape, jnp.float32)],
    )
    parts_shape = (shape[0] // window_rhs.shape[0],) + window_rhs.shape
    parts = call(last_kernel, parts_shape, where, other, sofar, *split, solve)
    return jnp.sum(lax.all_to_all(parts, "prow", 0, 0), axis=0)


def solution(mesh):
    placed = (P(("prow", "pcol"), None), P("prow", "pcol"), P("prow", "pcol"), P(), P())
    return jax.shard_map(
        body, mesh=mesh, in_specs=placed, out_specs=P("prow", "pcol"), check_vma=False
    )
```

```python
import jax
import jax.numpy as jnp
from jax import lax
from jax.experimental import pallas as pl
from jax.experimental.pallas import tpu as pltpu
from jax.sharding import PartitionSpec as P

STRIDE = 4
WINDOW_FLOPS = 10_000_000_000
PARAMS = pltpu.CompilerParams(vmem_limit_bytes=20 << 20)


def plain_product(left, right):
    return jnp.dot(left, right, precision=lax.Precision.HIGHEST, preferred_element_type=jnp.float32)


def halves(array):
    high = array.astype(jnp.bfloat16)
    return high, (array - high.astype(jnp.float32)).astype(jnp.bfloat16)


def three_passes(rows, right_high, right_low):
    left_high, left_low = halves(rows.T)
    total = jnp.dot(left_high, right_high, preferred_element_type=jnp.float32)
    total += jnp.dot(left_high, right_low, preferred_element_type=jnp.float32)
    return total + jnp.dot(left_low, right_high, preferred_element_type=jnp.float32)


def first_kernel(where, rows, tiles, coupling, inverses, out, own_high, own_low, other_high, other_low, solve):
    core = where[4]
    part = three_passes(rows[...], *halves(tiles[where[0], core]))

    @pl.when(pl.program_id(0) == 0)
    def _():
        out[...] = part
        upper, lower = inverses[0], inverses[1]
        carried = -plain_product(lower, plain_product(coupling[...], upper))
        top = jnp.concatenate([upper.T, carried.T], axis=1)
        bottom = jnp.concatenate([jnp.zeros_like(lower), lower.T], axis=1)
        solve[...] = jnp.concatenate([top, bottom], axis=0)

    @pl.when(pl.program_id(0) > 0)
    def _():
        out[...] += part

    for index in range(STRIDE):
        if index:
            own_high[index - 1], own_low[index - 1] = halves(tiles[where[index], core])
        other_high[index], other_low[index] = halves(tiles[where[index], 1 - core])


def first_product(where, rows, tiles, coupling, inverses):
    far, _, cores, panel_rows, columns = tiles.shape
    panel_columns = rows.shape[1]

    def whole(shape):
        return pl.BlockSpec(shape, lambda h, s: (0,) * len(shape))

    def split(count):
        shape = jax.ShapeDtypeStruct((count, far * panel_rows, columns), jnp.bfloat16)
        return [shape] * 2, [pl.BlockSpec((count, panel_rows, columns), lambda h, s: (0, h, 0))] * 2

    own_shapes, own_specs = split(STRIDE - 1)
    other_shapes, other_specs = split(STRIDE)
    product, square = (panel_columns, columns), (panel_columns, panel_columns)
    return pl.pallas_call(
        first_kernel,
        out_shape=[jax.ShapeDtypeStruct(product, jnp.float32)]
        + own_shapes
        + other_shapes
        + [jax.ShapeDtypeStruct(square, jnp.float32)],
        grid_spec=pltpu.PrefetchScalarGridSpec(
            num_scalar_prefetch=1,
            grid=(far,),
            in_specs=[
                pl.BlockSpec((panel_rows, panel_columns), lambda h, s: (h, 0)),
                pl.BlockSpec((None, STRIDE, cores, panel_rows, columns), lambda h, s: (h, 0, 0, 0, 0)),
                whole(coupling.shape),
                whole(inverses.shape),
            ],
            out_specs=[whole(product)] + own_specs + other_specs + [whole(square)],
        ),
        compiler_params=PARAMS,
        cost_estimate=pl.CostEstimate(flops=WINDOW_FLOPS, bytes_accessed=8 << 20, transcendentals=0),
    )(where, rows, tiles, coupling, inverses)


def call(kernel, out_shape, where, *arrays, scratch=()):
    return pl.pallas_call(
        kernel,
        out_shape=jax.ShapeDtypeStruct(out_shape, jnp.float32),
        in_specs=[pl.BlockSpec(memory_space=pltpu.SMEM)] + [pl.BlockSpec(memory_space=pltpu.VMEM)] * len(arrays),
        scratch_shapes=scratch,
        compiler_params=PARAMS,
        cost_estimate=pl.CostEstimate(flops=3 << 26, bytes_accessed=1 << 20, transcendentals=0),
    )(where, *arrays)


def middle_kernel(where, up, down, away, sofar, own_high, own_low, rhs, solve, out, total):
    share_rows = rhs.shape[0]
    total[...] = -sofar[...]
    for index, rows in enumerate((up, down, away)):
        total[...] -= three_passes(rows[...], own_high[index], own_low[index])
    at = pl.ds(pl.multiple_of(where[5] * share_rows, share_rows), share_rows)
    total[at, :] += rhs[...]
    out[...] = plain_product(solve[...], total[...])


def last_kernel(where, rows, sofar, other_high, other_low, solve, out):
    columns = sofar.shape[1]
    right = [half[...].reshape(-1, columns) for half in (other_high, other_low)]
    update = three_passes(rows[...], *right)
    out[...] = (sofar[...] - plain_product(solve[...], update)).reshape(out.shape)


def body(panel, solved, window_rhs, coupling, inverses):
    share_rows, columns = window_rhs.shape
    panel_rows, panel_columns = panel.shape
    grid_columns = lax.axis_size("pcol")
    chips = grid_columns // 2
    far = chips // STRIDE
    row_index = lax.axis_index("prow")
    column_index = lax.axis_index("pcol")
    place = (column_index // 2) % STRIDE
    tiles = solved.reshape(far, STRIDE, 2, panel_rows, columns)
    tiles, coupling, inverses = (
        pltpu.with_memory_space_constraint(array, pltpu.HBM) for array in (tiles, coupling, inverses)
    )

    def shifted(array, up, down):
        pairs = [(2 * z + c, 2 * ((z + (up, down)[c]) % chips) + c) for z in range(chips) for c in range(2)]
        return lax.ppermute(array, "pcol", pairs)

    def swapped(array):
        return lax.ppermute(array, "pcol", [(i, i ^ 1) for i in range(grid_columns)])

    groups = [[2 * (STRIDE * h + l) + c for h in range(far)] for l in range(STRIDE) for c in range(2)]
    own = lax.all_gather(panel, "pcol", axis=0, axis_index_groups=groups, tiled=True)
    first = shifted(own, 1, -1)
    second = shifted(own, -1, 1)
    away = shifted(own, 2, -2)
    core = column_index % 2
    below, above = (place + STRIDE - 1) % STRIDE, (place + 1) % STRIDE
    firsts = [jnp.where(core == 0, below, above), jnp.where(core == 0, above, below)]
    where = jnp.stack([place, *firsts, (place + 2) % STRIDE, core, row_index]).astype(jnp.int32)
    work = first_product(where, own, tiles, coupling, inverses)
    first, second, away, work = lax.optimization_barrier((first, second, away, work))
    sofar, own_high, own_low, other_high, other_low, solve = work
    other = swapped(jnp.concatenate([own, second, first, away]))
    shape = sofar.shape
    sofar = call(
        middle_kernel, shape, where, first, second, away, sofar, own_high, own_low, window_rhs, solve,
        scratch=[pltpu.VMEM(shape, jnp.float32)],
    )
    parts_shape = (shape[0] // share_rows, share_rows, columns)
    parts = call(last_kernel, parts_shape, where, other, sofar, other_high, other_low, solve)
    return jnp.sum(lax.all_to_all(parts, "prow", 0, 0), axis=0)


def solution(mesh):
    placed = (P(("prow", "pcol"), None), P("prow", "pcol"), P("prow", "pcol"), P(), P())
    return jax.shard_map(
        body, mesh=mesh, in_specs=placed, out_specs=P("prow", "pcol"), check_vma=False
    )
```

```python
import jax
import jax.numpy as jnp
from jax import lax
from jax.experimental import pallas as pl
from jax.experimental.pallas import tpu as pltpu
from jax.sharding import PartitionSpec as P

STRIDE = 4
WINDOW_FLOPS = 10_000_000_000
PARAMS = pltpu.CompilerParams(vmem_limit_bytes=20 << 20)


def plain_product(left, right):
    return jnp.dot(left, right, precision=lax.Precision.HIGHEST, preferred_element_type=jnp.float32)


def halves(array):
    high = array.astype(jnp.bfloat16)
    return high, (array - high.astype(jnp.float32)).astype(jnp.bfloat16)


def three_passes(rows, right_high, right_low):
    left_high, left_low = halves(rows.T)
    total = jnp.dot(left_high, right_high, preferred_element_type=jnp.float32)
    total += jnp.dot(left_high, right_low, preferred_element_type=jnp.float32)
    return total + jnp.dot(left_low, right_high, preferred_element_type=jnp.float32)


def split_kernel(where, tiles, coupling, inverses, high, low, solve, held, sems):
    far, stride, cores = tiles.shape[:3]
    copies = [pltpu.make_async_copy(tiles.at[h], held.at[h], sems.at[h]) for h in range(far)]
    for copy in copies:
        copy.start()
    upper, lower = inverses[0], inverses[1]
    carried = -plain_product(lower, plain_product(coupling[...], upper))
    top = jnp.concatenate([upper.T, carried.T], axis=1)
    bottom = jnp.concatenate([jnp.zeros_like(lower), lower.T], axis=1)
    solve[...] = jnp.concatenate([top, bottom], axis=0)
    for h in range(far):
        copies[h].wait()

        def one(index, _, h=h):
            at = (h, index // cores, index % cores)
            high[at], low[at] = halves(held[at])
            return 0

        lax.fori_loop(0, stride * cores, one, 0)


def split(where, tiles, coupling, inverses):
    block_rows = coupling.shape[0]
    half = jax.ShapeDtypeStruct(tiles.shape, jnp.bfloat16)
    vmem = pl.BlockSpec(memory_space=pltpu.VMEM)
    return pl.pallas_call(
        split_kernel,
        out_shape=[half, half, jax.ShapeDtypeStruct((2 * block_rows, 2 * block_rows), jnp.float32)],
        in_specs=[pl.BlockSpec(memory_space=pltpu.SMEM), pl.BlockSpec(memory_space=pltpu.HBM), vmem, vmem],
        out_specs=[vmem] * 3,
        scratch_shapes=[pltpu.VMEM(tiles.shape, jnp.float32), pltpu.SemaphoreType.DMA(tiles.shape[:1])],
        compiler_params=PARAMS,
        cost_estimate=pl.CostEstimate(flops=WINDOW_FLOPS, bytes_accessed=8 << 20, transcendentals=0),
    )(where, tiles, coupling, inverses)


def call(kernel, out_shape, where, *arrays, scratch=()):
    return pl.pallas_call(
        kernel,
        out_shape=jax.ShapeDtypeStruct(out_shape, jnp.float32),
        in_specs=[pl.BlockSpec(memory_space=pltpu.SMEM)] + [pl.BlockSpec(memory_space=pltpu.VMEM)] * len(arrays),
        scratch_shapes=scratch,
        compiler_params=PARAMS,
        cost_estimate=pl.CostEstimate(flops=3 << 26, bytes_accessed=1 << 20, transcendentals=0),
    )(where, *arrays)


def product(rows, where, index, core, high, low):
    at = (slice(None), where[index], core)
    columns = high.shape[-1]
    return three_passes(rows, high[at].reshape(-1, columns), low[at].reshape(-1, columns))


def first_kernel(where, rows, high, low, out):
    out[...] = product(rows[...], where, 0, where[4], high, low)


def middle_kernel(where, both, up, down, away, sofar, high, low, rhs, solve, out, total):
    share_rows = rhs.shape[0]
    core = where[4]
    total[...] = -sofar[...] - product(both[1 - core], where, 0, 1 - core, high, low)
    for index, rows in enumerate((up, down, away)):
        total[...] -= product(rows[...], where, index + 1, core, high, low)
    at = pl.ds(pl.multiple_of(where[5] * share_rows, share_rows), share_rows)
    total[at, :] += rhs[...]
    out[...] = plain_product(solve[...], total[...])


def last_kernel(where, rows, sofar, high, low, solve, out):
    depth = rows.shape[0] // 3
    other = 1 - where[4]
    update = product(rows[0:depth, :], where, 1, other, high, low)
    update += product(rows[depth : 2 * depth, :], where, 2, other, high, low)
    update += product(rows[2 * depth :, :], where, 3, other, high, low)
    out[...] = (sofar[...] - plain_product(solve[...], update)).reshape(out.shape)


def body(panel, solved, window_rhs, coupling, inverses):
    share_rows, columns = window_rhs.shape
    panel_rows, panel_columns = panel.shape
    grid_columns = lax.axis_size("pcol")
    chips = grid_columns // 2
    far = chips // STRIDE
    row_index = lax.axis_index("prow")
    column_index = lax.axis_index("pcol")
    place = (column_index // 2) % STRIDE
    tiles = solved.reshape(far, STRIDE, 2, panel_rows, columns)
    tiles, coupling, inverses = (
        pltpu.with_memory_space_constraint(array, pltpu.HBM) for array in (tiles, coupling, inverses)
    )

    def shifted(array, up, down):
        pairs = [(2 * z + c, 2 * ((z + (up, down)[c]) % chips) + c) for z in range(chips) for c in range(2)]
        return lax.ppermute(array, "pcol", pairs)

    def swapped(array):
        return lax.ppermute(array, "pcol", [(i, i ^ 1) for i in range(grid_columns)])

    groups = [[2 * (STRIDE * h + l) + c for h in range(far)] for l in range(STRIDE) for c in range(2)]
    own = lax.all_gather(panel, "pcol", axis=0, axis_index_groups=groups, tiled=True)
    first = shifted(own, 1, -1)
    second = shifted(own, -1, 1)
    away = shifted(own, 2, -2)
    core = column_index % 2
    below, above = (place + STRIDE - 1) % STRIDE, (place + 1) % STRIDE
    firsts = [jnp.where(core == 0, below, above), jnp.where(core == 0, above, below)]
    where = jnp.stack([place, *firsts, (place + 2) % STRIDE, core, row_index]).astype(jnp.int32)
    own, where = lax.optimization_barrier((own, where))
    high, low, solve = split(where, tiles, coupling, inverses)
    own, solve = lax.optimization_barrier((own, solve))
    chip = [[2 * z, 2 * z + 1] for z in range(chips)]
    both = lax.all_gather(own, "pcol", axis=0, axis_index_groups=chip)
    shape = (panel_columns, columns)
    sofar = call(first_kernel, shape, where, own, high, low)
    first, second, away, both, sofar = lax.optimization_barrier((first, second, away, both, sofar))
    other = swapped(jnp.concatenate([second, first, away]))
    sofar = call(
        middle_kernel, shape, where, both, first, second, away, sofar, high, low, window_rhs, solve,
        scratch=[pltpu.VMEM(shape, jnp.float32)],
    )
    parts_shape = (shape[0] // share_rows, share_rows, columns)
    parts = call(last_kernel, parts_shape, where, other, sofar, high, low, solve)
    return jnp.sum(lax.all_to_all(parts, "prow", 0, 0), axis=0)


def solution(mesh):
    placed = (P(("prow", "pcol"), None), P("prow", "pcol"), P("prow", "pcol"), P(), P())
    return jax.shard_map(
        body, mesh=mesh, in_specs=placed, out_specs=P("prow", "pcol"), check_vma=False
    )
```

```python
import jax
import jax.numpy as jnp
from jax import lax
from jax.experimental import pallas as pl
from jax.experimental.pallas import tpu as pltpu
from jax.sharding import PartitionSpec as P

STRIDE = 4
WINDOW_FLOPS = 10_000_000_000
PARAMS = pltpu.CompilerParams(vmem_limit_bytes=20 << 20)


def plain_product(left, right):
    return jnp.dot(left, right, precision=lax.Precision.HIGHEST, preferred_element_type=jnp.float32)


def halves(array):
    high = array.astype(jnp.bfloat16)
    return high, (array - high.astype(jnp.float32)).astype(jnp.bfloat16)


def three_passes(rows, right_high, right_low):
    left_high, left_low = halves(rows.T)
    both = jnp.dot(jnp.concatenate([left_high, left_low]), right_high, preferred_element_type=jnp.float32)
    count = left_high.shape[0]
    return both[:count] + both[count:] + jnp.dot(left_high, right_low, preferred_element_type=jnp.float32)


def split_kernel(where, tiles, coupling, inverses, high, low, solve, held, sems):
    far, stride, cores = tiles.shape[:3]
    copies = [pltpu.make_async_copy(tiles.at[h], held.at[h], sems.at[h]) for h in range(far)]
    for copy in copies:
        copy.start()
    upper, lower = inverses[0], inverses[1]
    carried = -plain_product(lower, plain_product(coupling[...], upper))
    top = jnp.concatenate([upper.T, carried.T], axis=1)
    bottom = jnp.concatenate([jnp.zeros_like(lower), lower.T], axis=1)
    solve[...] = jnp.concatenate([top, bottom], axis=0)
    for h in range(far):
        copies[h].wait()

        def one(index, _, h=h):
            at = (h, index // cores, index % cores)
            high[at], low[at] = halves(held[at])
            return 0

        lax.fori_loop(0, stride * cores, one, 0)


def split(where, tiles, coupling, inverses):
    block_rows = coupling.shape[0]
    half = jax.ShapeDtypeStruct(tiles.shape, jnp.bfloat16)
    vmem = pl.BlockSpec(memory_space=pltpu.VMEM)
    return pl.pallas_call(
        split_kernel,
        out_shape=[half, half, jax.ShapeDtypeStruct((2 * block_rows, 2 * block_rows), jnp.float32)],
        in_specs=[pl.BlockSpec(memory_space=pltpu.SMEM), pl.BlockSpec(memory_space=pltpu.HBM), vmem, vmem],
        out_specs=[vmem] * 3,
        scratch_shapes=[pltpu.VMEM(tiles.shape, jnp.float32), pltpu.SemaphoreType.DMA(tiles.shape[:1])],
        compiler_params=PARAMS,
        cost_estimate=pl.CostEstimate(flops=WINDOW_FLOPS, bytes_accessed=8 << 20, transcendentals=0),
    )(where, tiles, coupling, inverses)


def call(kernel, out_shape, where, *arrays, scratch=()):
    return pl.pallas_call(
        kernel,
        out_shape=jax.ShapeDtypeStruct(out_shape, jnp.float32),
        in_specs=[pl.BlockSpec(memory_space=pltpu.SMEM)] + [pl.BlockSpec(memory_space=pltpu.VMEM)] * len(arrays),
        scratch_shapes=scratch,
        compiler_params=PARAMS,
        cost_estimate=pl.CostEstimate(flops=3 << 26, bytes_accessed=1 << 20, transcendentals=0),
    )(where, *arrays)


def product(rows, where, index, core, high, low):
    at = (slice(None), where[index], core)
    columns = high.shape[-1]
    return three_passes(rows, high[at].reshape(-1, columns), low[at].reshape(-1, columns))


def first_kernel(where, rows, high, low, out):
    out[...] = product(rows[...], where, 0, where[4], high, low)


def middle_kernel(where, both, up, down, away, sofar, high, low, rhs, solve, out, total):
    share_rows = rhs.shape[0]
    core = where[4]
    total[...] = -sofar[...] - product(both[1 - core], where, 0, 1 - core, high, low)
    for index, rows in enumerate((up, down, away)):
        total[...] -= product(rows[...], where, index + 1, core, high, low)
    at = pl.ds(pl.multiple_of(where[5] * share_rows, share_rows), share_rows)
    total[at, :] += rhs[...]
    out[...] = plain_product(solve[...], total[...])


def last_kernel(where, rows, sofar, high, low, solve, out):
    depth = rows.shape[0] // 3
    other = 1 - where[4]
    update = product(rows[0:depth, :], where, 1, other, high, low)
    update += product(rows[depth : 2 * depth, :], where, 2, other, high, low)
    update += product(rows[2 * depth :, :], where, 3, other, high, low)
    out[...] = (sofar[...] - plain_product(solve[...], update)).reshape(out.shape)


def body(panel, solved, window_rhs, coupling, inverses):
    share_rows, columns = window_rhs.shape
    panel_rows, panel_columns = panel.shape
    grid_columns = lax.axis_size("pcol")
    chips = grid_columns // 2
    far = chips // STRIDE
    row_index = lax.axis_index("prow")
    column_index = lax.axis_index("pcol")
    place = (column_index // 2) % STRIDE
    tiles = solved.reshape(far, STRIDE, 2, panel_rows, columns)
    tiles, coupling, inverses = (
        pltpu.with_memory_space_constraint(array, pltpu.HBM) for array in (tiles, coupling, inverses)
    )

    def shifted(array, up, down):
        pairs = [(2 * z + c, 2 * ((z + (up, down)[c]) % chips) + c) for z in range(chips) for c in range(2)]
        return lax.ppermute(array, "pcol", pairs)

    def swapped(array):
        return lax.ppermute(array, "pcol", [(i, i ^ 1) for i in range(grid_columns)])

    groups = [[2 * (STRIDE * h + l) + c for h in range(far)] for l in range(STRIDE) for c in range(2)]
    own = lax.all_gather(panel, "pcol", axis=0, axis_index_groups=groups, tiled=True)
    first = shifted(own, 1, -1)
    second = shifted(own, -1, 1)
    away = shifted(own, 2, -2)
    core = column_index % 2
    below, above = (place + STRIDE - 1) % STRIDE, (place + 1) % STRIDE
    firsts = [jnp.where(core == 0, below, above), jnp.where(core == 0, above, below)]
    where = jnp.stack([place, *firsts, (place + 2) % STRIDE, core, row_index]).astype(jnp.int32)
    own, where = lax.optimization_barrier((own, where))
    high, low, solve = split(where, tiles, coupling, inverses)
    own, solve = lax.optimization_barrier((own, solve))
    chip = [[2 * z, 2 * z + 1] for z in range(chips)]
    both = lax.all_gather(own, "pcol", axis=0, axis_index_groups=chip)
    shape = (panel_columns, columns)
    sofar = call(first_kernel, shape, where, own, high, low)
    first, second, away, both, sofar = lax.optimization_barrier((first, second, away, both, sofar))
    other = swapped(jnp.concatenate([second, first, away]))
    sofar = call(
        middle_kernel, shape, where, both, first, second, away, sofar, high, low, window_rhs, solve,
        scratch=[pltpu.VMEM(shape, jnp.float32)],
    )
    parts_shape = (shape[0] // share_rows, share_rows, columns)
    parts = call(last_kernel, parts_shape, where, other, sofar, high, low, solve)
    return jnp.sum(lax.all_to_all(parts, "prow", 0, 0), axis=0)


def solution(mesh):
    placed = (P(("prow", "pcol"), None), P("prow", "pcol"), P("prow", "pcol"), P(), P())
    return jax.shard_map(
        body, mesh=mesh, in_specs=placed, out_specs=P("prow", "pcol"), check_vma=False
    )
```

```python
import jax
import jax.numpy as jnp
from jax import lax
from jax.experimental import pallas as pl
from jax.experimental.pallas import tpu as pltpu
from jax.sharding import PartitionSpec as P

STRIDE = 4
WINDOW_FLOPS = 10_000_000_000
PARAMS = pltpu.CompilerParams(vmem_limit_bytes=20 << 20)


def plain_product(left, right):
    return jnp.dot(left, right, precision=lax.Precision.HIGHEST, preferred_element_type=jnp.float32)


def halves(array):
    high = array.astype(jnp.bfloat16)
    return high, (array - high.astype(jnp.float32)).astype(jnp.bfloat16)


def three_passes(rows, right_high, right_low):
    left_high, left_low = halves(rows.T)
    both = jnp.dot(jnp.concatenate([left_high, left_low]), right_high, preferred_element_type=jnp.float32)
    count = left_high.shape[0]
    return both[:count] + both[count:] + jnp.dot(left_high, right_low, preferred_element_type=jnp.float32)


def solved_product(solve, array):
    left_high, left_low = halves(solve)
    right_high, right_low = halves(array)
    both = jnp.dot(jnp.concatenate([left_high, left_low]), right_high, preferred_element_type=jnp.float32)
    count = left_high.shape[0]
    return both[:count] + both[count:] + jnp.dot(left_high, right_low, preferred_element_type=jnp.float32)


def split_kernel(where, tiles, coupling, inverses, high, low, solve, held, sems):
    far, stride, cores = tiles.shape[:3]
    copies = [pltpu.make_async_copy(tiles.at[h], held.at[h], sems.at[h]) for h in range(far)]
    for copy in copies:
        copy.start()
    upper, lower = inverses[0], inverses[1]
    carried = -plain_product(lower, plain_product(coupling[...], upper))
    top = jnp.concatenate([upper.T, carried.T], axis=1)
    bottom = jnp.concatenate([jnp.zeros_like(lower), lower.T], axis=1)
    solve[...] = jnp.concatenate([top, bottom], axis=0)
    for h in range(far):
        copies[h].wait()

        def one(index, _, h=h):
            at = (h, index // cores, index % cores)
            high[at], low[at] = halves(held[at])
            return 0

        lax.fori_loop(0, stride * cores, one, 0)


def split(where, tiles, coupling, inverses):
    block_rows = coupling.shape[0]
    half = jax.ShapeDtypeStruct(tiles.shape, jnp.bfloat16)
    vmem = pl.BlockSpec(memory_space=pltpu.VMEM)
    return pl.pallas_call(
        split_kernel,
        out_shape=[half, half, jax.ShapeDtypeStruct((2 * block_rows, 2 * block_rows), jnp.float32)],
        in_specs=[pl.BlockSpec(memory_space=pltpu.SMEM), pl.BlockSpec(memory_space=pltpu.HBM), vmem, vmem],
        out_specs=[vmem] * 3,
        scratch_shapes=[pltpu.VMEM(tiles.shape, jnp.float32), pltpu.SemaphoreType.DMA(tiles.shape[:1])],
        compiler_params=PARAMS,
        cost_estimate=pl.CostEstimate(flops=WINDOW_FLOPS, bytes_accessed=8 << 20, transcendentals=0),
    )(where, tiles, coupling, inverses)


def call(kernel, out_shape, where, *arrays, scratch=()):
    return pl.pallas_call(
        kernel,
        out_shape=jax.ShapeDtypeStruct(out_shape, jnp.float32),
        in_specs=[pl.BlockSpec(memory_space=pltpu.SMEM)] + [pl.BlockSpec(memory_space=pltpu.VMEM)] * len(arrays),
        scratch_shapes=scratch,
        compiler_params=PARAMS,
        cost_estimate=pl.CostEstimate(flops=3 << 26, bytes_accessed=1 << 20, transcendentals=0),
    )(where, *arrays)


def product(rows, where, index, core, high, low):
    at = (slice(None), where[index], core)
    columns = high.shape[-1]
    return three_passes(rows, high[at].reshape(-1, columns), low[at].reshape(-1, columns))


def first_kernel(where, rows, high, low, out):
    out[...] = product(rows[...], where, 0, where[4], high, low)


def middle_kernel(where, both, up, down, away, sofar, high, low, rhs, solve, out, total):
    share_rows = rhs.shape[0]
    core = where[4]
    total[...] = -sofar[...] - product(both[1 - core], where, 0, 1 - core, high, low)
    for index, rows in enumerate((up, down, away)):
        total[...] -= product(rows[...], where, index + 1, core, high, low)
    at = pl.ds(pl.multiple_of(where[5] * share_rows, share_rows), share_rows)
    total[at, :] += rhs[...]
    out[...] = solved_product(solve[...], total[...])


def last_kernel(where, rows, sofar, high, low, solve, out):
    depth = rows.shape[0] // 3
    other = 1 - where[4]
    update = product(rows[0:depth, :], where, 1, other, high, low)
    update += product(rows[depth : 2 * depth, :], where, 2, other, high, low)
    update += product(rows[2 * depth :, :], where, 3, other, high, low)
    out[...] = (sofar[...] - solved_product(solve[...], update)).reshape(out.shape)


def body(panel, solved, window_rhs, coupling, inverses):
    share_rows, columns = window_rhs.shape
    panel_rows, panel_columns = panel.shape
    grid_columns = lax.axis_size("pcol")
    chips = grid_columns // 2
    far = chips // STRIDE
    row_index = lax.axis_index("prow")
    column_index = lax.axis_index("pcol")
    place = (column_index // 2) % STRIDE
    tiles = solved.reshape(far, STRIDE, 2, panel_rows, columns)
    tiles, coupling, inverses = (
        pltpu.with_memory_space_constraint(array, pltpu.HBM) for array in (tiles, coupling, inverses)
    )

    def shifted(array, up, down):
        pairs = [(2 * z + c, 2 * ((z + (up, down)[c]) % chips) + c) for z in range(chips) for c in range(2)]
        return lax.ppermute(array, "pcol", pairs)

    def swapped(array):
        return lax.ppermute(array, "pcol", [(i, i ^ 1) for i in range(grid_columns)])

    groups = [[2 * (STRIDE * h + l) + c for h in range(far)] for l in range(STRIDE) for c in range(2)]
    own = lax.all_gather(panel, "pcol", axis=0, axis_index_groups=groups, tiled=True)
    first = shifted(own, 1, -1)
    second = shifted(own, -1, 1)
    away = shifted(own, 2, -2)
    core = column_index % 2
    below, above = (place + STRIDE - 1) % STRIDE, (place + 1) % STRIDE
    firsts = [jnp.where(core == 0, below, above), jnp.where(core == 0, above, below)]
    where = jnp.stack([place, *firsts, (place + 2) % STRIDE, core, row_index]).astype(jnp.int32)
    own, where = lax.optimization_barrier((own, where))
    high, low, solve = split(where, tiles, coupling, inverses)
    own, solve = lax.optimization_barrier((own, solve))
    chip = [[2 * z, 2 * z + 1] for z in range(chips)]
    both = lax.all_gather(own, "pcol", axis=0, axis_index_groups=chip)
    shape = (panel_columns, columns)
    sofar = call(first_kernel, shape, where, own, high, low)
    first, second, away, both, sofar = lax.optimization_barrier((first, second, away, both, sofar))
    other = swapped(jnp.concatenate([second, first, away]))
    sofar = call(
        middle_kernel, shape, where, both, first, second, away, sofar, high, low, window_rhs, solve,
        scratch=[pltpu.VMEM(shape, jnp.float32)],
    )
    parts_shape = (shape[0] // share_rows, share_rows, columns)
    parts = call(last_kernel, parts_shape, where, other, sofar, high, low, solve)
    return jnp.sum(lax.all_to_all(parts, "prow", 0, 0), axis=0)


def solution(mesh):
    placed = (P(("prow", "pcol"), None), P("prow", "pcol"), P("prow", "pcol"), P(), P())
    return jax.shard_map(
        body, mesh=mesh, in_specs=placed, out_specs=P("prow", "pcol"), check_vma=False
    )
```

```python
import jax
import jax.numpy as jnp
from jax import lax
from jax.experimental import pallas as pl
from jax.experimental.pallas import tpu as pltpu
from jax.sharding import PartitionSpec as P

STRIDE = 4
WINDOW_FLOPS = 10_000_000_000
PARAMS = pltpu.CompilerParams(vmem_limit_bytes=20 << 20)


def plain_product(left, right):
    return jnp.dot(left, right, precision=lax.Precision.HIGHEST, preferred_element_type=jnp.float32)


def halves(array):
    high = array.astype(jnp.bfloat16)
    return high, (array - high.astype(jnp.float32)).astype(jnp.bfloat16)


def three_passes(rows, right_high, right_low):
    left_high, left_low = halves(rows.T)
    both = jnp.dot(jnp.concatenate([left_high, left_low]), right_high, preferred_element_type=jnp.float32)
    count = left_high.shape[0]
    return both[:count] + both[count:] + jnp.dot(left_high, right_low, preferred_element_type=jnp.float32)


def solved_product(solve, array):
    left_high, left_low = halves(solve)
    right_high, right_low = halves(array)
    both = jnp.dot(jnp.concatenate([left_high, left_low]), right_high, preferred_element_type=jnp.float32)
    count = left_high.shape[0]
    return both[:count] + both[count:] + jnp.dot(left_high, right_low, preferred_element_type=jnp.float32)


def split_kernel(where, tiles, coupling, inverses, high, low, solve, held, sems):
    far, stride, cores = tiles.shape[:3]
    copies = [pltpu.make_async_copy(tiles.at[h], held.at[h], sems.at[h]) for h in range(far)]
    for copy in copies:
        copy.start()
    upper, lower = inverses[0], inverses[1]
    carried = -plain_product(lower, plain_product(coupling[...], upper))
    top = jnp.concatenate([upper.T, carried.T], axis=1)
    bottom = jnp.concatenate([jnp.zeros_like(lower), lower.T], axis=1)
    solve[...] = jnp.concatenate([top, bottom], axis=0)
    for h in range(far):
        copies[h].wait()

        def one(index, _, h=h):
            at = (h, index // cores, index % cores)
            high[at], low[at] = halves(held[at])
            return 0

        lax.fori_loop(0, stride * cores, one, 0)


def split(where, tiles, coupling, inverses):
    block_rows = coupling.shape[0]
    half = jax.ShapeDtypeStruct(tiles.shape, jnp.bfloat16)
    vmem = pl.BlockSpec(memory_space=pltpu.VMEM)
    return pl.pallas_call(
        split_kernel,
        out_shape=[half, half, jax.ShapeDtypeStruct((2 * block_rows, 2 * block_rows), jnp.float32)],
        in_specs=[pl.BlockSpec(memory_space=pltpu.SMEM), pl.BlockSpec(memory_space=pltpu.HBM), vmem, vmem],
        out_specs=[vmem] * 3,
        scratch_shapes=[pltpu.VMEM(tiles.shape, jnp.float32), pltpu.SemaphoreType.DMA(tiles.shape[:1])],
        compiler_params=PARAMS,
        cost_estimate=pl.CostEstimate(flops=WINDOW_FLOPS, bytes_accessed=8 << 20, transcendentals=0),
    )(where, tiles, coupling, inverses)


def call(kernel, out_shape, where, *arrays, scratch=()):
    return pl.pallas_call(
        kernel,
        out_shape=jax.ShapeDtypeStruct(out_shape, jnp.float32),
        in_specs=[pl.BlockSpec(memory_space=pltpu.SMEM)] + [pl.BlockSpec(memory_space=pltpu.VMEM)] * len(arrays),
        scratch_shapes=scratch,
        compiler_params=PARAMS,
        cost_estimate=pl.CostEstimate(flops=3 << 26, bytes_accessed=1 << 20, transcendentals=0),
    )(where, *arrays)


def product(rows, where, index, core, high, low):
    at = (slice(None), where[index], core)
    columns = high.shape[-1]
    return three_passes(rows, high[at].reshape(-1, columns), low[at].reshape(-1, columns))


def first_kernel(where, rows, high, low, out):
    out[...] = product(rows[...], where, 0, where[4], high, low)


def middle_kernel(where, both, up, down, away, sofar, high, low, rhs, solve, out, total):
    share_rows = rhs.shape[0]
    core = where[4]
    total[...] = -sofar[...] - product(both[1 - core], where, 0, 1 - core, high, low)
    for index, rows in enumerate((up, down, away)):
        total[...] -= product(rows[...], where, index + 1, core, high, low)
    at = pl.ds(pl.multiple_of(where[5] * share_rows, share_rows), share_rows)
    total[at, :] += rhs[...]
    out[...] = solved_product(solve[...], total[...])


def last_kernel(where, rows, sofar, high, low, solve, out):
    depth = rows.shape[0] // 3
    other = 1 - where[4]
    update = product(rows[0:depth, :], where, 1, other, high, low)
    update += product(rows[depth : 2 * depth, :], where, 2, other, high, low)
    update += product(rows[2 * depth :, :], where, 3, other, high, low)
    out[...] = (sofar[...] - solved_product(solve[...], update)).reshape(out.shape)


def body(panel, solved, window_rhs, coupling, inverses):
    share_rows, columns = window_rhs.shape
    panel_rows, panel_columns = panel.shape
    grid_columns = lax.axis_size("pcol")
    chips = grid_columns // 2
    far = chips // STRIDE
    row_index = lax.axis_index("prow")
    column_index = lax.axis_index("pcol")
    place = (column_index // 2) % STRIDE
    tiles = solved.reshape(far, STRIDE, 2, panel_rows, columns)
    tiles, coupling, inverses = (
        pltpu.with_memory_space_constraint(array, pltpu.HBM) for array in (tiles, coupling, inverses)
    )

    def shifted(array, up, down):
        pairs = [(2 * z + c, 2 * ((z + (up, down)[c]) % chips) + c) for z in range(chips) for c in range(2)]
        return lax.ppermute(array, "pcol", pairs)

    def exchanged(array, odd):
        pairs = [(2 * z + c, 2 * ((((z + odd) ^ 1) - odd) % chips) + c) for z in range(chips) for c in range(2)]
        return lax.ppermute(array, "pcol", pairs)

    def swapped(array):
        return lax.ppermute(array, "pcol", [(i, i ^ 1) for i in range(grid_columns)])

    groups = [[2 * (STRIDE * h + l) + c for h in range(far)] for l in range(STRIDE) for c in range(2)]
    own = lax.all_gather(panel, "pcol", axis=0, axis_index_groups=groups, tiled=True)
    first = exchanged(own, 0)
    second = exchanged(own, 1)
    away = shifted(own, 2, -2)
    places = [place, place ^ 1, place ^ 3, place ^ 2]
    where = jnp.stack([*places, column_index % 2, row_index]).astype(jnp.int32)
    own, where = lax.optimization_barrier((own, where))
    high, low, solve = split(where, tiles, coupling, inverses)
    own, solve = lax.optimization_barrier((own, solve))
    chip = [[2 * z, 2 * z + 1] for z in range(chips)]
    both = lax.all_gather(own, "pcol", axis=0, axis_index_groups=chip)
    shape = (panel_columns, columns)
    sofar = call(first_kernel, shape, where, own, high, low)
    first, second, away, both, sofar = lax.optimization_barrier((first, second, away, both, sofar))
    other = swapped(jnp.concatenate([first, second, away]))
    sofar = call(
        middle_kernel, shape, where, both, first, second, away, sofar, high, low, window_rhs, solve,
        scratch=[pltpu.VMEM(shape, jnp.float32)],
    )
    parts_shape = (shape[0] // share_rows, share_rows, columns)
    parts = call(last_kernel, parts_shape, where, other, sofar, high, low, solve)
    return jnp.sum(lax.all_to_all(parts, "prow", 0, 0), axis=0)


def solution(mesh):
    placed = (P(("prow", "pcol"), None), P("prow", "pcol"), P("prow", "pcol"), P(), P())
    return jax.shard_map(
        body, mesh=mesh, in_specs=placed, out_specs=P("prow", "pcol"), check_vma=False
    )
```
